32 devices in a mesh: gx: 8 (over y, x, core), gy: 4 (over z).
Axes of the slice: x: 2, y: 2, z: 4, core: 2. Of those that a mesh axis runs over, the one named last changes fastest.
Arguments:
- field: float32 [32, 128, 1024], P('gx', 'gy'), may hold values from -6 to 6
- cotangent: float32 [32, 128, 1024], P('gx', 'gy'), may hold values from -6 to 6
- spectral_weight: float32 [32, 32, 2, 32, 512], P('gx', None, None, None, 'gy'), may hold values from -6 to 6
- point_weight: float32 [32, 32], replicated, may hold values from -1 to 1
- point_bias: float32 [32], replicated, may hold values from -3 to 3
Outputs:
- output: float32 [32, 128, 1024], P('gx', 'gy')
- grad_field: float32 [32, 128, 1024], P('gx', 'gy')
- grad_spectral: float32 [32, 32, 2, 32, 512], P('gx', None, None, None, 'gy')
- grad_point: float32 [32, 32], replicated
- grad_bias: float32 [32], replicated
The draws below stay inside these ranges and needn't reach their ends.
All inputs are finite; a program needn't handle non-finite values.
Results may differ from the reference program's by a relative error of at most 0.00013.
Values sent between devices are 32-bit elements; how exact they have to be, the bound alone decides.
A program may use at most 128 MiB of HBM per device.

```python
import math
import jax
import jax.numpy as jnp
from jax import lax

C = 32
KX = 32
KY = 32
KZ = 16
NZ = 32
NX = 32
NY = 128


def level_of(stream_key, extent, shards, smallest, top_value):
    def one(axis_at, parts):
        heights = jax.random.uniform(jax.random.fold_in(jax.random.fold_in(stream_key, 6), axis_at), (parts,), jnp.float32, smallest / len(shards), top_value / len(shards))
        return jnp.repeat(jnp.exp(heights), extent[axis_at] // parts).reshape((-1,) + (1,) * (len(extent) - axis_at - 1))

    loudness = one(*shards[0])
    for cut in shards[1:]:
        loudness = loudness * one(*cut)
    return loudness


def gaussian(stream_key, extent, scale, most, cuts=(), kind=jnp.bfloat16):
    loudness = level_of(stream_key, extent, cuts, -0.22, 0.18) if cuts else 1.0
    result = jax.random.normal(stream_key, extent, jnp.float32) * scale * loudness
    return jnp.minimum(jnp.maximum(result, -most), most).astype(kind)


def setup_inputs(seed: int = 0) -> dict:
    key_of = jax.random.split(jax.random.key(seed), 6)
    field = gaussian(key_of[0], (NX, NY, NZ * C), 1.0, 6.0, ((0, 8), (1, 4)), jnp.float32)
    cotangent = gaussian(key_of[1], (NX, NY, NZ * C), 1.0, 6.0, ((0, 8), (1, 4)), jnp.float32)
    spectral_weight = gaussian(key_of[2], (KY, KX, 2, C, KZ * C), 1.0, 6.0, ((0, 8), (4, 4)), jnp.float32)
    point_weight = gaussian(key_of[3], (C, C), C ** -0.5, 1.0, (), jnp.float32)
    point_bias = gaussian(key_of[4], (C,), 0.5, 3.0, (), jnp.float32)
    return {"field": field, "cotangent": cotangent, "spectral_weight": spectral_weight, "point_weight": point_weight, "point_bias": point_bias}


HIGH = lax.Precision.HIGHEST

def phase_table(positions, length, modes, signed):
    index = jnp.arange(modes, dtype=jnp.int32)
    if signed:
        frequency = jnp.where(index >= modes // 2, index - modes, index)
    else:
        frequency = index
    turns = jnp.mod(positions[:, None] * frequency[None, :], length).astype(jnp.float32) * (2.0 * math.pi / length)
    return (jnp.cos(turns), jnp.sin(turns))

def contract(form, left, right):
    return jnp.einsum(form, left, right, precision=HIGH)

def all_tables():
    cos_x, sin_x = phase_table(jnp.arange(NX, dtype=jnp.int32), NX, KX, True)
    cos_y, sin_y = phase_table(jnp.arange(NY, dtype=jnp.int32), NY, KY, True)
    cos_z, sin_z = phase_table(jnp.arange(NZ, dtype=jnp.int32), NZ, KZ, False)
    return (cos_x, sin_x, cos_y, sin_y, cos_z, sin_z)

def analyse(signal):
    cos_x, sin_x, cos_y, sin_y, cos_z, sin_z = all_tables()
    z_real = contract('xyzc,zk->xykc', signal, cos_z)
    z_imag = -contract('xyzc,zk->xykc', signal, sin_z)
    y_real = contract('xykc,yq->xqkc', z_real, cos_y) + contract('xykc,yq->xqkc', z_imag, sin_y)
    y_imag = contract('xykc,yq->xqkc', z_imag, cos_y) - contract('xykc,yq->xqkc', z_real, sin_y)
    x_real = contract('xqkc,xp->qpkc', y_real, cos_x) + contract('xqkc,xp->qpkc', y_imag, sin_x)
    x_imag = contract('xqkc,xp->qpkc', y_imag, cos_x) - contract('xqkc,xp->qpkc', y_real, sin_x)
    return (x_real, x_imag)

def synthesise(x_real, x_imag):
    cos_x, sin_x, cos_y, sin_y, cos_z, sin_z = all_tables()
    back_real = contract('qpkc,xp->xqkc', x_real, cos_x) - contract('qpkc,xp->xqkc', x_imag, sin_x)
    back_imag = contract('qpkc,xp->xqkc', x_real, sin_x) + contract('qpkc,xp->xqkc', x_imag, cos_x)
    grid_real = contract('xqkc,yq->xykc', back_real, cos_y) - contract('xqkc,yq->xykc', back_imag, sin_y)
    grid_imag = contract('xqkc,yq->xykc', back_real, sin_y) + contract('xqkc,yq->xykc', back_imag, cos_y)
    return contract('xykc,zk->xyzc', grid_real, cos_z) - contract('xykc,zk->xyzc', grid_imag, sin_z)

def layer(field, spectral_weight, point_weight, point_bias):
    signal = field.reshape(NX, NY, NZ, C)
    spec_real, spec_imag = analyse(signal)
    weight_real = spectral_weight[:, :, 0].reshape(KY, KX, C, KZ, C)
    weight_imag = spectral_weight[:, :, 1].reshape(KY, KX, C, KZ, C)
    mixed_real = contract('qpki,qpiko->qpko', spec_real, weight_real) - contract('qpki,qpiko->qpko', spec_imag, weight_imag)
    mixed_imag = contract('qpki,qpiko->qpko', spec_real, weight_imag) + contract('qpki,qpiko->qpko', spec_imag, weight_real)
    factor = (jnp.where(jnp.arange(KZ) == 0, 1.0, 2.0) / (NX * NY * NZ)).astype(jnp.float32)[:, None]
    spectral = synthesise(mixed_real * factor, mixed_imag * factor)
    hidden = spectral + contract('xyzi,io->xyzo', signal, point_weight) + point_bias
    return jax.nn.gelu(hidden, approximate=False).reshape(NX, NY, NZ * C)

def reference(field, cotangent, spectral_weight, point_weight, point_bias):
    output, pullback = jax.vjp(layer, field, spectral_weight, point_weight, point_bias)
    grad_field, grad_spectral, grad_point, grad_bias = pullback(cotangent)
    root = math.sqrt(NX * NY * NZ)
    return (output, grad_field, grad_spectral, grad_point / root, grad_bias / root)
```

```python
import functools
import math

import jax
import jax.numpy as jnp
import ml_dtypes
import numpy as np
from jax import lax
from jax.experimental import pallas as pl
from jax.experimental.pallas import tpu as pltpu
from jax.sharding import PartitionSpec as P

F32 = jnp.float32
BF16 = jnp.bfloat16
MESH = pl.DeviceIdType.MESH
HIGHEST = lax.Precision.HIGHEST
WIDE = 256
ROWS = 8
VMEM_BYTES = 58 * 1024 * 1024


def phases(positions, length, modes, signed):
    index = np.arange(modes)
    frequency = np.where(index >= modes // 2, index - modes, index) if signed else index
    turns = np.mod(positions[:, None] * frequency[None, :], length) * (2.0 * math.pi / length)
    return np.cos(turns), np.sin(turns)


def halves(table):
    table = np.asarray(table, np.float32)
    high = table.astype(ml_dtypes.bfloat16)
    low = (table - high.astype(np.float32)).astype(ml_dtypes.bfloat16)
    return high, low


def thirds(table):
    high, low = halves(table)
    return np.concatenate([high, high, low], -1)


def tables(nx, ny, nz, kx, ky, kz, chan, owned, split_y):
    cos_z, sin_z = phases(np.arange(nz), nz, kz, False)
    eye = np.eye(chan)
    first = np.concatenate([np.kron(cos_z, eye), np.kron(-sin_z, eye)], 1)
    cos_y, sin_y = phases(np.arange(ny), ny, ky, True)
    cells = ny // split_y
    cos_y = cos_y.reshape(split_y, cells, ky).transpose(0, 2, 1)
    sin_y = sin_y.reshape(split_y, cells, ky).transpose(0, 2, 1)
    real = np.concatenate([cos_y, sin_y], 2)
    imag = np.concatenate([-sin_y, cos_y], 2)
    second = np.stack([real, imag], 2).reshape(split_y, 2 * ky, 2 * cells)
    cos_x, sin_x = phases(np.arange(nx), nx, kx, True)
    third = np.zeros((owned, 2, kx, nx, owned, 2))
    for q in range(owned):
        third[q, 0, :, :, q, 0] = cos_x.T
        third[q, 0, :, :, q, 1] = sin_x.T
        third[q, 1, :, :, q, 0] = -sin_x.T
        third[q, 1, :, :, q, 1] = cos_x.T
    third = third.reshape(owned * 2 * kx, nx * owned * 2)
    return (
        *halves(first),
        *halves(first.T),
        thirds(second),
        thirds(second.transpose(0, 2, 1)),
        *halves(third),
        *halves(third.T),
    )


def parts_of(value):
    high = value.astype(BF16)
    return high, (value - high.astype(F32)).astype(BF16)


def dot(left, right):
    return jnp.dot(left, right, preferred_element_type=F32)


def right_product(value, high_table, low_table):
    rows = value.shape[0]
    high, low = parts_of(value)
    both = dot(jnp.concatenate([high, low], 0), high_table)
    return both[:rows] + both[rows:] + dot(high, low_table)


def left_product(high_table, low_table, value):
    columns = value.shape[1]
    high, low = parts_of(value)
    both = dot(high_table, jnp.concatenate([high, low], 1))
    return both[:, :columns] + both[:, columns:] + dot(low_table, high)


def left_thirds(table, value):
    high, low = parts_of(value)
    return dot(table, jnp.concatenate([high, low, high], 0))


def exact(left, right, dims):
    return lax.dot_general(
        left, right, (dims, ((), ())), precision=HIGHEST, preferred_element_type=F32
    )


def iota(shape, axis):
    return lax.broadcasted_iota(jnp.int32, shape, axis)


def kernel(
    sizes,
    field, cotangent, weight_in, point, bias,
    za_high, za_low, zs_high_in, zs_low_in, ya, ys, xa_high, xa_low, xs_high, xs_low,
    output, grad_field, grad_weight_out, grad_point, grad_bias,
    weight, zs_high, zs_low, spread_real, spread_imag, grad_weight, hidden_base, grad_hidden,
    coefficients, mixed,
    rs_out, rs_in, xy_out, xy_in, yx_out, yx_in, gathered, total_y, total_x,
    rs_ss, rs_rs, xy_ss, xy_rs, yx_ss, yx_rs, ag_ss, ag_rs, ty_ss, ty_rs, tx_ss, tx_rs, local_sem, out_sem,
):
    A, B, CX, CY, KX, KC, L, C, owned, cells, steps = sizes
    R2 = 2 * owned
    a = lax.axis_index("gx")
    b = lax.axis_index("gy")

    def peer_x(d):
        return lax.rem(a + d, A)

    def peer_y(d):
        return lax.rem(b + d, B)

    def place(gx, gy):
        return {"gx": gx, "gy": gy}

    def remote(src, dst, ss, rs, where):
        return pltpu.make_async_remote_copy(
            src_ref=src, dst_ref=dst, send_sem=ss, recv_sem=rs, device_id=where, device_id_type=MESH
        )

    barrier = pltpu.get_barrier_semaphore()
    for d in range(1, A):
        pl.semaphore_signal(barrier, inc=1, device_id=place(peer_x(d), b), device_id_type=MESH)
    for d in range(1, B):
        pl.semaphore_signal(barrier, inc=1, device_id=place(a, peer_y(d)), device_id_type=MESH)
    loads = [
        pltpu.make_async_copy(weight_in, weight, local_sem.at[0]),
        pltpu.make_async_copy(zs_high_in, zs_high, local_sem.at[1]),
        pltpu.make_async_copy(zs_low_in, zs_low, local_sem.at[2]),
    ]
    for load in loads:
        load.start()
    sends = []

    def analyse_columns(turn, rows, first):
        z = right_product(rows, za_high[...], za_low[...])
        for n in range(rows.shape[0] // CY):
            one = z[n * CY : (n + 1) * CY]
            y = left_thirds(ya[b], jnp.concatenate([one[:, :KC], one[:, KC:]], 0))
            for j in range(B):
                rs_out[turn, j, first + n] = y[:, j * L : (j + 1) * L]

    def scatter(turn, x):
        made = []
        for d in range(1, B):
            copy = remote(
                rs_out.at[turn, peer_y(d), x], rs_in.at[turn, d, x],
                rs_ss.at[turn, d, x], rs_rs.at[turn, d, x], place(a, peer_y(d)),
            )
            copy.start()
            made.append(copy)
        sends.extend(made)
        return made

    def sum_and_send(turn, first, count, arriving):
        for n in range(count):
            x = first + n
            total = rs_out[turn, b, x]
            for d, copy in enumerate(arriving[x], 1):
                copy.wait_recv()
                total = total + rs_in[turn, d, x]
            for s in range(A):
                xy_out[turn, s, x] = total[s * R2 : (s + 1) * R2]
        h = first // count
        made = []
        for d in range(1, A):
            copy = remote(
                xy_out.at[turn, peer_x(d), pl.ds(first, count)], xy_in.at[turn, a, pl.ds(first, count)],
                xy_ss.at[turn, d, h], xy_rs.at[turn, d, h], place(peer_x(d), b),
            )
            copy.start()
            made.append(copy)
        sends.extend(made)
        xy_in[turn, a, pl.ds(first, count)] = xy_out[turn, a, pl.ds(first, count)]
        return made

    def transform_x(turn, arriving):
        for copy in arriving:
            copy.wait_recv()
        if R2 % ROWS == 0:
            value = xy_in[turn].reshape(A * CX * R2, L)
        else:
            value = jnp.concatenate([xy_in[turn, s, x] for s in range(A) for x in range(CX)], 0)
        return left_product(xa_high[...], xa_low[...], value)

    def back_x(turn):
        value = left_product(xs_high[...], xs_low[...], mixed[...])
        for s in range(A):
            for x in range(CX):
                at = (s * CX + x) * R2
                yx_out[turn, s, x] = value[at : at + R2]
        made = []
        for d in range(1, A):
            copy = remote(
                yx_out.at[turn, peer_x(d)], yx_in.at[turn, a],
                yx_ss.at[turn, d], yx_rs.at[turn, d], place(peer_x(d), b),
            )
            copy.start()
            made.append(copy)
        sends.extend(made)
        yx_in[turn, a] = yx_out[turn, a]
        return made

    def gather(turn, arriving):
        for copy in arriving:
            copy.wait_recv()
        made = []
        count = CX // steps
        for h in range(steps):
            for x in range(h * count, (h + 1) * count):
                for s in range(A):
                    gathered[turn, b, x, s * R2 : (s + 1) * R2] = yx_in[turn, s, x]
            own = gathered.at[turn, b, pl.ds(h * count, count)]
            group = []
            for d in range(1, B):
                copy = remote(
                    own, own, ag_ss.at[turn, d, h], ag_rs.at[turn, d, h], place(a, peer_y(d))
                )
                copy.start()
                group.append(copy)
            sends.extend(group)
            made.append(group)
        return made

    def synthesise_columns(turn, first, count, arriving):
        for copy in arriving:
            copy.wait_recv()
        slabs = []
        for x in range(first, first + count):
            modes = jnp.concatenate([gathered[turn, j, x] for j in range(B)], 1)
            grid = left_thirds(ys[b], modes)
            slabs.append(jnp.concatenate([grid[:CY], grid[CY:]], 1))
        return right_product(jnp.concatenate(slabs, 0), zs_high[...], zs_low[...])

    fold = (iota((WIDE, C), 0) % C == iota((WIDE, C), 1)).astype(F32)
    fold_wide = (iota((WIDE, L), 0) % C == iota((WIDE, L), 1)).astype(F32)
    same = (iota((WIDE, WIDE), 0) // C == iota((WIDE, WIDE), 1) // C).astype(F32)
    pick = (iota((C, L), 0) == iota((C, L), 1) % C).astype(F32)
    group = ((iota((2 * L, L), 0) % L) // C == iota((2 * L, L), 1) // C).astype(F32).astype(BF16)
    mode = b * (L // C) + iota((1, L), 1) // C
    factor = jnp.where(mode == 0, 1.0, 2.0).astype(F32) * (1.0 / cells)
    columns = field.shape[2]
    blocks = columns // WIDE

    def stacked(value):
        return jnp.concatenate([value[:, j * WIDE : (j + 1) * WIDE] for j in range(blocks)], 0)

    def unstacked(value):
        rows = value.shape[0] // blocks
        return jnp.concatenate([value[j * rows : (j + 1) * rows] for j in range(blocks)], 1)

    def pointwise(value, axis):
        table = exact(exact(fold, point[...], ((1,), (axis,))), fold, ((1,), (1,))) * same
        return unstacked(right_product(stacked(value), *parts_of(table)))

    signal = field[...].reshape(CX * CY, columns)
    analyse_columns(0, signal, 0)
    pl.semaphore_wait(barrier, A + B - 2)
    arriving = [scatter(0, x) for x in range(CX)]
    tiled = exact(bias[...], fold, ((1,), (1,)))
    hidden_base[...] = pointwise(signal, 0) + jnp.concatenate([tiled] * blocks, 1)
    count = CX // steps
    moved = []
    for h in range(steps):
        moved += sum_and_send(0, h * count, count, arriving)
    coefficients[...] = transform_x(0, moved)
    loads[0].wait()
    per = KX // ROWS

    def place_of(t):
        q = t // per
        p = (t % per) * ROWS
        return q, p, pl.multiple_of(q * (2 * KX) + p, ROWS)

    def grouped(high, low):
        return dot(jnp.concatenate([high, low], 1), group)

    def widen(value):
        high, low = parts_of(value)
        pair = [
            (part.astype(F32)[:, None, :] * pick[None]).reshape(ROWS * C, L).astype(BF16)
            for part in (high, low)
        ]
        return grouped(*pair).reshape(ROWS, C, L)

    def mix(t, carry):
        q, p, at = place_of(t)
        real = widen(coefficients[pl.ds(at, ROWS)])
        imag = widen(coefficients[pl.ds(at + KX, ROWS)])
        spread_real[q, pl.ds(p, ROWS)] = real
        spread_imag[q, pl.ds(p, ROWS)] = imag
        w_real = weight[q, pl.ds(p, ROWS), 0]
        w_imag = weight[q, pl.ds(p, ROWS), 1]
        mixed[pl.ds(at, ROWS)] = jnp.sum(real * w_real - imag * w_imag, 1) * factor
        mixed[pl.ds(at + KX, ROWS)] = jnp.sum(real * w_imag + imag * w_real, 1) * factor
        return carry

    lax.fori_loop(0, owned * per, mix, 0)
    returned = gather(0, back_x(0))
    loads[1].wait()
    loads[2].wait()

    arriving = []
    for h in range(steps):
        rows = count * CY
        at = h * rows
        value = synthesise_columns(0, h * count, count, returned[h]) + hidden_base[at : at + rows]
        below = 0.5 * (1.0 + lax.erf(value * math.sqrt(0.5)))
        density = jnp.exp(-0.5 * value * value) * (1.0 / math.sqrt(2.0 * math.pi))
        output[h * count : (h + 1) * count] = (value * below).reshape(count, CY, columns)
        upper = cotangent[h * count : (h + 1) * count].reshape(rows, columns)
        slope = upper * (below + value * density)
        grad_hidden[at : at + rows] = slope
        analyse_columns(1, slope, h * count)
        arriving += [scatter(1, h * count + n) for n in range(count)]

    slope = grad_hidden[...]
    left = parts_of(stacked(field[...].reshape(CX * CY, columns)))
    right = parts_of(stacked(slope))

    def crossed(one, two):
        return lax.dot_general(one, two, (((0,), (0,)), ((), ())), preferred_element_type=F32)

    pairs = (crossed(left[0], right[0]) + crossed(left[0], right[1]) + crossed(left[1], right[0])) * same
    point_part = exact(exact(fold, pairs, ((0,), (0,))), fold_wide, ((1,), (0,)))
    bias_part = exact(jnp.sum(stacked(slope), 0, keepdims=True), fold_wide, ((1,), (0,)))
    total_y[b, 0:C] = point_part
    total_y[b, C : C + ROWS] = jnp.broadcast_to(bias_part, (ROWS, L))
    own = total_y.at[b]
    totals = []
    for d in range(1, B):
        copy = remote(own, own, ty_ss.at[d], ty_rs.at[d], place(a, peer_y(d)))
        copy.start()
        totals.append(copy)
    sends.extend(totals)
    hidden_base[...] = pointwise(slope, 1)

    moved = []
    for h in range(steps):
        moved += sum_and_send(1, h * count, count, arriving)
    for copy in totals:
        copy.wait_recv()
    total = total_y[0]
    for j in range(1, B):
        total = total + total_y[j]
    total_x[a] = total
    own = total_x.at[a]
    totals = []
    for d in range(1, A):
        copy = remote(own, own, tx_ss.at[d], tx_rs.at[d], place(peer_x(d), b))
        copy.start()
        totals.append(copy)
    sends.extend(totals)
    coefficients[...] = transform_x(1, moved) * factor

    def unmix(t, carry):
        q, p, at = place_of(t)
        real = coefficients[pl.ds(at, ROWS)][:, None, :]
        imag = coefficients[pl.ds(at + KX, ROWS)][:, None, :]
        w_real = weight[q, pl.ds(p, ROWS), 0]
        w_imag = weight[q, pl.ds(p, ROWS), 1]
        for term, to in ((real * w_real + imag * w_imag, at), (imag * w_real - real * w_imag, at + KX)):
            summed = grouped(*parts_of(term.reshape(ROWS * C, L))).reshape(ROWS, C, L)
            mixed[pl.ds(to, ROWS)] = jnp.sum(summed * pick[None], 1)
        return carry

    lax.fori_loop(0, owned * per, unmix, 0)
    back = back_x(1)

    def weigh(t, carry):
        q, p, at = place_of(t)
        real = coefficients[pl.ds(at, ROWS)][:, None, :]
        imag = coefficients[pl.ds(at + KX, ROWS)][:, None, :]
        s_real = spread_real[q, pl.ds(p, ROWS)]
        s_imag = spread_imag[q, pl.ds(p, ROWS)]
        grad_weight[q, pl.ds(p, ROWS), 0] = s_real * real + s_imag * imag
        grad_weight[q, pl.ds(p, ROWS), 1] = s_real * imag - s_imag * real
        return carry

    returned = gather(1, back)
    lax.fori_loop(0, owned * per, weigh, 0)
    store = pltpu.make_async_copy(grad_weight, grad_weight_out, out_sem.at[0])
    store.start()
    for copy in totals:
        copy.wait_recv()
    total = total_x[0]
    for s in range(1, A):
        total = total + total_x[s]
    total = total * (1.0 / math.sqrt(cells))
    grad_point[...] = total[0:C, 0:C]
    grad_bias[...] = total[C : C + 1, 0:C]
    for h in range(steps):
        rows = count * CY
        at = h * rows
        value = synthesise_columns(1, h * count, count, returned[h]) + hidden_base[at : at + rows]
        grad_field[h * count : (h + 1) * count] = value.reshape(count, CY, columns)
    store.wait()
    for copy in sends:
        copy.wait_send()


def shards(A, B, field, cotangent, weight, point, bias):
    CX, CY, columns = field.shape
    C = point.shape[0]
    owned, KX, _, _, L = weight.shape
    depth = L // C
    KY, KZ, NZ = owned * A, depth * B, columns // C
    NX, NY = CX * A, CY * B
    cells = NX * NY * NZ
    R, R2, KC = 2 * KY, 2 * owned, KZ * C
    steps = 2 if CX % 2 == 0 else 1
    made = [jnp.asarray(t) for t in tables(NX, NY, NZ, KX, KY, KZ, C, owned, B)]
    sizes = (A, B, CX, CY, KX, KC, L, C, owned, cells, steps)
    vmem = pl.BlockSpec(memory_space=pltpu.VMEM)
    far = pl.BlockSpec(memory_space=pl.ANY)
    dma = pltpu.SemaphoreType.DMA
    z_shape = made[2].shape
    modes = owned * 2 * KX
    results = pl.pallas_call(
        functools.partial(kernel, sizes),
        out_shape=(
            jax.ShapeDtypeStruct(field.shape, F32),
            jax.ShapeDtypeStruct(field.shape, F32),
            jax.ShapeDtypeStruct(weight.shape, F32),
            jax.ShapeDtypeStruct((C, C), F32),
            jax.ShapeDtypeStruct((1, C), F32),
        ),
        in_specs=[vmem, vmem, far, vmem, vmem, vmem, vmem, far, far] + [vmem] * 6,
        out_specs=(vmem, vmem, far, vmem, vmem),
        scratch_shapes=[
            pltpu.VMEM(weight.shape, F32),
            pltpu.VMEM(z_shape, BF16),
            pltpu.VMEM(z_shape, BF16),
            pltpu.VMEM((owned, KX, C, L), F32),
            pltpu.VMEM((owned, KX, C, L), F32),
            pltpu.VMEM(weight.shape, F32),
            pltpu.VMEM((CX * CY, columns), F32),
            pltpu.VMEM((CX * CY, columns), F32),
            pltpu.VMEM((modes, L), F32),
            pltpu.VMEM((modes, L), F32),
            pltpu.VMEM((2, B, CX, R, L), F32),
            pltpu.VMEM((2, B, CX, R, L), F32),
            pltpu.VMEM((2, A, CX, R2, L), F32),
            pltpu.VMEM((2, A, CX, R2, L), F32),
            pltpu.VMEM((2, A, CX, R2, L), F32),
            pltpu.VMEM((2, A, CX, R2, L), F32),
            pltpu.VMEM((2, B, CX, R, L), F32),
            pltpu.VMEM((B, C + ROWS, L), F32),
            pltpu.VMEM((A, C + ROWS, L), F32),
            dma((2, B, CX)), dma((2, B, CX)),
            dma((2, A, steps)), dma((2, A, steps)),
            dma((2, A)), dma((2, A)),
            dma((2, B, steps)), dma((2, B, steps)),
            dma((B,)), dma((B,)),
            dma((A,)), dma((A,)),
            dma((3,)), dma((1,)),
        ],
        compiler_params=pltpu.CompilerParams(
            collective_id=0, has_side_effects=True, vmem_limit_bytes=VMEM_BYTES
        ),
    )(field, cotangent, weight, point, bias.reshape(1, C), *made)
    return (*results[:4], results[4].reshape(C))


def solution(mesh):
    placed = (P("gx", "gy", None), P("gx", "gy", None), P("gx", None, None, None, "gy"), P(), P())
    return jax.shard_map(
        functools.partial(shards, mesh.shape["gx"], mesh.shape["gy"]),
        mesh=mesh,
        in_specs=placed,
        out_specs=(
            P("gx", "gy", None),
            P("gx", "gy", None),
            P("gx", None, None, None, "gy"),
            P(),
            P(),
        ),
        check_vma=False,
    )
```

```python
import functools
import math

import jax
import jax.numpy as jnp
import ml_dtypes
import numpy as np
from jax import lax
from jax.experimental import pallas as pl
from jax.experimental.pallas import tpu as pltpu
from jax.sharding import PartitionSpec as P

F32 = jnp.float32
BF16 = jnp.bfloat16
MESH = pl.DeviceIdType.MESH
HIGHEST = lax.Precision.HIGHEST
WIDE = 256
ROWS = 8
VMEM_BYTES = 58 * 1024 * 1024


def phases(positions, length, modes, signed):
    index = np.arange(modes)
    frequency = np.where(index >= modes // 2, index - modes, index) if signed else index
    turns = np.mod(positions[:, None] * frequency[None, :], length) * (2.0 * math.pi / length)
    return np.cos(turns), np.sin(turns)


def halves(table):
    table = np.asarray(table, np.float32)
    high = table.astype(ml_dtypes.bfloat16)
    low = (table - high.astype(np.float32)).astype(ml_dtypes.bfloat16)
    return high, low


def thirds(table):
    high, low = halves(table)
    return np.concatenate([high, high, low], -1)


def tables(nx, ny, nz, kx, ky, kz, chan, owned, split_y):
    cos_z, sin_z = phases(np.arange(nz), nz, kz, False)
    eye = np.eye(chan)
    first = np.concatenate([np.kron(cos_z, eye), np.kron(-sin_z, eye)], 1)
    cos_y, sin_y = phases(np.arange(ny), ny, ky, True)
    cells = ny // split_y
    cos_y = cos_y.reshape(split_y, cells, ky).transpose(0, 2, 1)
    sin_y = sin_y.reshape(split_y, cells, ky).transpose(0, 2, 1)
    real = np.concatenate([cos_y, sin_y], 2)
    imag = np.concatenate([-sin_y, cos_y], 2)
    second = np.stack([real, imag], 2).reshape(split_y, 2 * ky, 2 * cells)
    cos_x, sin_x = phases(np.arange(nx), nx, kx, True)
    third = np.zeros((owned, 2, kx, nx, owned, 2))
    for q in range(owned):
        third[q, 0, :, :, q, 0] = cos_x.T
        third[q, 0, :, :, q, 1] = sin_x.T
        third[q, 1, :, :, q, 0] = -sin_x.T
        third[q, 1, :, :, q, 1] = cos_x.T
    third = third.reshape(owned * 2 * kx, nx * owned * 2)
    return (
        *halves(first),
        *halves(first.T),
        thirds(second),
        thirds(second.transpose(0, 2, 1)),
        *halves(third),
        *halves(third.T),
    )


def parts_of(value):
    high = value.astype(BF16)
    return high, (value - high.astype(F32)).astype(BF16)


def dot(left, right):
    return jnp.dot(left, right, preferred_element_type=F32)


def right_product(value, high_table, low_table):
    rows = value.shape[0]
    high, low = parts_of(value)
    both = dot(jnp.concatenate([high, low], 0), high_table)
    return both[:rows] + both[rows:] + dot(high, low_table)


def left_product(high_table, low_table, value):
    columns = value.shape[1]
    high, low = parts_of(value)
    both = dot(high_table, jnp.concatenate([high, low], 1))
    return both[:, :columns] + both[:, columns:] + dot(low_table, high)


def left_thirds(table, value):
    high, low = parts_of(value)
    return dot(table, jnp.concatenate([high, low, high], 0))


def exact(left, right, dims):
    return lax.dot_general(
        left, right, (dims, ((), ())), precision=HIGHEST, preferred_element_type=F32
    )


def iota(shape, axis):
    return lax.broadcasted_iota(jnp.int32, shape, axis)


def channel_tables(C, L):
    pick = (iota((C, L), 0) == iota((C, L), 1) % C).astype(F32)
    group = ((iota((2 * L, L), 0) % L) // C == iota((2 * L, L), 1) // C).astype(F32).astype(BF16)
    return pick, group


def grouped(high, low, group):
    return dot(jnp.concatenate([high, low], 1), group)


def widen(value, pick, group):
    C, L = pick.shape
    high, low = parts_of(value)
    pair = [
        (part.astype(F32)[:, None, :] * pick[None]).reshape(value.shape[0] * C, L).astype(BF16)
        for part in (high, low)
    ]
    return grouped(*pair, group).reshape(value.shape[0], C, L)


def finish(
    sizes, spectrum, slopes, output_in, field_in, point_in, bias_in,
    output, grad_field, grad_weight_out, grad_point, grad_bias, grad_weight, sem,
):
    owned, KX, C, L = sizes
    copies = [
        pltpu.make_async_copy(output_in, output, sem.at[owned]),
        pltpu.make_async_copy(field_in, grad_field, sem.at[owned + 1]),
    ]
    for copy in copies:
        copy.start()
    grad_point[...] = point_in[...]
    grad_bias[...] = bias_in[...]
    pick, group = channel_tables(C, L)
    for q in range(owned):
        for p in range(0, KX, ROWS):
            at = q * 2 * KX + p
            s_real = widen(spectrum[at : at + ROWS], pick, group)
            s_imag = widen(spectrum[at + KX : at + KX + ROWS], pick, group)
            real = slopes[at : at + ROWS][:, None, :]
            imag = slopes[at + KX : at + KX + ROWS][:, None, :]
            grad_weight[q, p : p + ROWS, 0] = s_real * real + s_imag * imag
            grad_weight[q, p : p + ROWS, 1] = s_real * imag - s_imag * real
        copy = pltpu.make_async_copy(grad_weight.at[q], grad_weight_out.at[q], sem.at[q])
        copy.start()
        copies.append(copy)
    for copy in copies:
        copy.wait()


def kernel(
    sizes,
    field, cotangent, weight_in, point, bias,
    za_high, za_low, zs_high_in, zs_low_in, ya, ys, xa_high, xa_low, xs_high, xs_low,
    output, grad_field, spectrum, slopes, grad_point, grad_bias,
    weight, zs_high, zs_low, hidden_base, grad_hidden, mixed,
    rs_out, rs_in, xy_out, xy_in, yx_out, yx_in, gathered, total_y, total_x,
    rs_ss, rs_rs, xy_ss, xy_rs, yx_ss, yx_rs, ag_ss, ag_rs, ty_ss, ty_rs, tx_ss, tx_rs, local_sem,
):
    A, B, CX, CY, KX, KC, L, C, owned, cells, steps = sizes
    R2 = 2 * owned
    a = lax.axis_index("gx")
    b = lax.axis_index("gy")

    def peer_x(d):
        return lax.rem(a + d, A)

    def peer_y(d):
        return lax.rem(b + d, B)

    def place(gx, gy):
        return {"gx": gx, "gy": gy}

    def remote(src, dst, ss, rs, where):
        return pltpu.make_async_remote_copy(
            src_ref=src, dst_ref=dst, send_sem=ss, recv_sem=rs, device_id=where, device_id_type=MESH
        )

    barrier = pltpu.get_barrier_semaphore()
    for d in range(1, A):
        pl.semaphore_signal(barrier, inc=1, device_id=place(peer_x(d), b), device_id_type=MESH)
    for d in range(1, B):
        pl.semaphore_signal(barrier, inc=1, device_id=place(a, peer_y(d)), device_id_type=MESH)
    loads = [
        pltpu.make_async_copy(weight_in, weight, local_sem.at[0]),
        pltpu.make_async_copy(zs_high_in, zs_high, local_sem.at[1]),
        pltpu.make_async_copy(zs_low_in, zs_low, local_sem.at[2]),
    ]
    for load in loads:
        load.start()
    sends = []

    def analyse_columns(turn, rows, first):
        z = right_product(rows, za_high[...], za_low[...])
        for n in range(rows.shape[0] // CY):
            one = z[n * CY : (n + 1) * CY]
            y = left_thirds(ya[b], jnp.concatenate([one[:, :KC], one[:, KC:]], 0))
            for j in range(B):
                rs_out[turn, j, first + n] = y[:, j * L : (j + 1) * L]

    def scatter(turn, x):
        made = []
        for d in range(1, B):
            copy = remote(
                rs_out.at[turn, peer_y(d), x], rs_in.at[turn, d, x],
                rs_ss.at[turn, d, x], rs_rs.at[turn, d, x], place(a, peer_y(d)),
            )
            copy.start()
            made.append(copy)
        sends.extend(made)
        return made

    def sum_and_send(turn, first, count, arriving):
        for n in range(count):
            x = first + n
            total = rs_out[turn, b, x]
            for d, copy in enumerate(arriving[x], 1):
                copy.wait_recv()
                total = total + rs_in[turn, d, x]
            for s in range(A):
                xy_out[turn, s, x] = total[s * R2 : (s + 1) * R2]
        h = first // count
        made = []
        for d in range(1, A):
            copy = remote(
                xy_out.at[turn, peer_x(d), pl.ds(first, count)], xy_in.at[turn, a, pl.ds(first, count)],
                xy_ss.at[turn, d, h], xy_rs.at[turn, d, h], place(peer_x(d), b),
            )
            copy.start()
            made.append(copy)
        sends.extend(made)
        xy_in[turn, a, pl.ds(first, count)] = xy_out[turn, a, pl.ds(first, count)]
        return made

    def transform_x(turn, arriving):
        for copy in arriving:
            copy.wait_recv()
        if R2 % ROWS == 0:
            value = xy_in[turn].reshape(A * CX * R2, L)
        else:
            value = jnp.concatenate([xy_in[turn, s, x] for s in range(A) for x in range(CX)], 0)
        return left_product(xa_high[...], xa_low[...], value)

    def back_x(turn):
        value = left_product(xs_high[...], xs_low[...], mixed[...])
        for s in range(A):
            for x in range(CX):
                at = (s * CX + x) * R2
                yx_out[turn, s, x] = value[at : at + R2]
        made = []
        for d in range(1, A):
            copy = remote(
                yx_out.at[turn, peer_x(d)], yx_in.at[turn, a],
                yx_ss.at[turn, d], yx_rs.at[turn, d], place(peer_x(d), b),
            )
            copy.start()
            made.append(copy)
        sends.extend(made)
        yx_in[turn, a] = yx_out[turn, a]
        return made

    def gather(turn, arriving):
        for copy in arriving:
            copy.wait_recv()
        made = []
        count = CX // steps
        for h in range(steps):
            for x in range(h * count, (h + 1) * count):
                for s in range(A):
                    gathered[turn, b, x, s * R2 : (s + 1) * R2] = yx_in[turn, s, x]
            own = gathered.at[turn, b, pl.ds(h * count, count)]
            group = []
            for d in range(1, B):
                copy = remote(
                    own, own, ag_ss.at[turn, d, h], ag_rs.at[turn, d, h], place(a, peer_y(d))
                )
                copy.start()
                group.append(copy)
            sends.extend(group)
            made.append(group)
        return made

    def synthesise_columns(turn, first, count, arriving):
        for copy in arriving:
            copy.wait_recv()
        slabs = []
        for x in range(first, first + count):
            modes = jnp.concatenate([gathered[turn, j, x] for j in range(B)], 1)
            grid = left_thirds(ys[b], modes)
            slabs.append(jnp.concatenate([grid[:CY], grid[CY:]], 1))
        return right_product(jnp.concatenate(slabs, 0), zs_high[...], zs_low[...])

    fold = (iota((WIDE, C), 0) % C == iota((WIDE, C), 1)).astype(F32)
    fold_wide = (iota((WIDE, L), 0) % C == iota((WIDE, L), 1)).astype(F32)
    same = (iota((WIDE, WIDE), 0) // C == iota((WIDE, WIDE), 1) // C).astype(F32)
    pick, group = channel_tables(C, L)
    mode = b * (L // C) + iota((1, L), 1) // C
    factor = jnp.where(mode == 0, 1.0, 2.0).astype(F32) * (1.0 / cells)
    columns = field.shape[2]
    blocks = columns // WIDE

    def stacked(value):
        return jnp.concatenate([value[:, j * WIDE : (j + 1) * WIDE] for j in range(blocks)], 0)

    def unstacked(value):
        rows = value.shape[0] // blocks
        return jnp.concatenate([value[j * rows : (j + 1) * rows] for j in range(blocks)], 1)

    def pointwise(value, axis):
        table = exact(exact(fold, point[...], ((1,), (axis,))), fold, ((1,), (1,))) * same
        return unstacked(right_product(stacked(value), *parts_of(table)))

    signal = field[...].reshape(CX * CY, columns)
    count = CX // steps
    rows = count * CY
    arriving = []
    for h in range(steps):
        analyse_columns(0, signal[h * rows : (h + 1) * rows], h * count)
        if h == 0:
            pl.semaphore_wait(barrier, A + B - 2)
        arriving += [scatter(0, h * count + n) for n in range(count)]
    tiled = exact(bias[...], fold, ((1,), (1,)))
    hidden_base[...] = pointwise(signal, 0) + jnp.concatenate([tiled] * blocks, 1)
    moved = []
    for h in range(steps):
        moved += sum_and_send(0, h * count, count, arriving)
    spectrum[...] = transform_x(0, moved)
    loads[0].wait()
    per = KX // ROWS

    def place_of(t):
        q = t // per
        p = (t % per) * ROWS
        return q, p, pl.multiple_of(q * (2 * KX) + p, ROWS)

    def over_modes(step):
        many = max(n for n in (4, 2, 1) if (owned * per) % n == 0)

        def some(t, carry):
            for n in range(many):
                step(t * many + n)
            return carry

        lax.fori_loop(0, owned * per // many, some, 0)

    def mix(t):
        q, p, at = place_of(t)
        real = widen(spectrum[pl.ds(at, ROWS)], pick, group)
        imag = widen(spectrum[pl.ds(at + KX, ROWS)], pick, group)
        w_real = weight[q, pl.ds(p, ROWS), 0]
        w_imag = weight[q, pl.ds(p, ROWS), 1]
        mixed[pl.ds(at, ROWS)] = jnp.sum(real * w_real - imag * w_imag, 1) * factor
        mixed[pl.ds(at + KX, ROWS)] = jnp.sum(real * w_imag + imag * w_real, 1) * factor

    over_modes(mix)
    returned = gather(0, back_x(0))
    loads[1].wait()
    loads[2].wait()

    arriving = []
    for h in range(steps):
        rows = count * CY
        at = h * rows
        value = synthesise_columns(0, h * count, count, returned[h]) + hidden_base[at : at + rows]
        below = 0.5 * (1.0 + lax.erf(value * math.sqrt(0.5)))
        density = jnp.exp(-0.5 * value * value) * (1.0 / math.sqrt(2.0 * math.pi))
        output[h * count : (h + 1) * count] = (value * below).reshape(count, CY, columns)
        upper = cotangent[h * count : (h + 1) * count].reshape(rows, columns)
        slope = upper * (below + value * density)
        grad_hidden[at : at + rows] = slope
        analyse_columns(1, slope, h * count)
        arriving += [scatter(1, h * count + n) for n in range(count)]

    slope = grad_hidden[...]
    left = parts_of(stacked(field[...].reshape(CX * CY, columns)))
    right = parts_of(stacked(slope))

    def crossed(one, two):
        return lax.dot_general(one, two, (((0,), (0,)), ((), ())), preferred_element_type=F32)

    pairs = (crossed(left[0], right[0]) + crossed(left[0], right[1]) + crossed(left[1], right[0])) * same
    point_part = exact(exact(fold, pairs, ((0,), (0,))), fold_wide, ((1,), (0,)))
    bias_part = exact(jnp.sum(stacked(slope), 0, keepdims=True), fold_wide, ((1,), (0,)))
    total_y[b, 0:C] = point_part
    total_y[b, C : C + ROWS] = jnp.broadcast_to(bias_part, (ROWS, L))
    own = total_y.at[b]
    totals = []
    for d in range(1, B):
        copy = remote(own, own, ty_ss.at[d], ty_rs.at[d], place(a, peer_y(d)))
        copy.start()
        totals.append(copy)
    sends.extend(totals)
    hidden_base[...] = pointwise(slope, 1)

    moved = []
    for h in range(steps):
        moved += sum_and_send(1, h * count, count, arriving)
    for copy in totals:
        copy.wait_recv()
    total = total_y[0]
    for j in range(1, B):
        total = total + total_y[j]
    total_x[a] = total
    own = total_x.at[a]
    totals = []
    for d in range(1, A):
        copy = remote(own, own, tx_ss.at[d], tx_rs.at[d], place(peer_x(d), b))
        copy.start()
        totals.append(copy)
    sends.extend(totals)
    slopes[...] = transform_x(1, moved) * factor

    def unmix(t):
        q, p, at = place_of(t)
        real = slopes[pl.ds(at, ROWS)][:, None, :]
        imag = slopes[pl.ds(at + KX, ROWS)][:, None, :]
        w_real = weight[q, pl.ds(p, ROWS), 0]
        w_imag = weight[q, pl.ds(p, ROWS), 1]
        for term, to in ((real * w_real + imag * w_imag, at), (imag * w_real - real * w_imag, at + KX)):
            summed = grouped(*parts_of(term.reshape(ROWS * C, L)), group).reshape(ROWS, C, L)
            mixed[pl.ds(to, ROWS)] = jnp.sum(summed * pick[None], 1)

    over_modes(unmix)
    returned = gather(1, back_x(1))
    for copy in totals:
        copy.wait_recv()
    total = total_x[0]
    for s in range(1, A):
        total = total + total_x[s]
    total = total * (1.0 / math.sqrt(cells))
    grad_point[...] = total[0:C, 0:C]
    grad_bias[...] = total[C : C + 1, 0:C]
    for h in range(steps):
        rows = count * CY
        at = h * rows
        value = synthesise_columns(1, h * count, count, returned[h]) + hidden_base[at : at + rows]
        grad_field[h * count : (h + 1) * count] = value.reshape(count, CY, columns)
    for copy in sends:
        copy.wait_send()


def shards(A, B, field, cotangent, weight, point, bias):
    CX, CY, columns = field.shape
    C = point.shape[0]
    owned, KX, _, _, L = weight.shape
    depth = L // C
    KY, KZ, NZ = owned * A, depth * B, columns // C
    NX, NY = CX * A, CY * B
    cells = NX * NY * NZ
    R, R2, KC = 2 * KY, 2 * owned, KZ * C
    steps = 2 if CX % 2 == 0 else 1
    made = [jnp.asarray(t) for t in tables(NX, NY, NZ, KX, KY, KZ, C, owned, B)]
    sizes = (A, B, CX, CY, KX, KC, L, C, owned, cells, steps)
    vmem = pl.BlockSpec(memory_space=pltpu.VMEM)
    far = pl.BlockSpec(memory_space=pl.ANY)
    dma = pltpu.SemaphoreType.DMA
    z_shape = made[2].shape
    modes = owned * 2 * KX
    output, grad_field, spectrum, slopes, grad_point, grad_bias = pl.pallas_call(
        functools.partial(kernel, sizes),
        out_shape=(
            jax.ShapeDtypeStruct(field.shape, F32),
            jax.ShapeDtypeStruct(field.shape, F32),
            jax.ShapeDtypeStruct((modes, L), F32),
            jax.ShapeDtypeStruct((modes, L), F32),
            jax.ShapeDtypeStruct((C, C), F32),
            jax.ShapeDtypeStruct((1, C), F32),
        ),
        in_specs=[vmem, vmem, far, vmem, vmem, vmem, vmem, far, far] + [vmem] * 6,
        out_specs=(vmem,) * 6,
        scratch_shapes=[
            pltpu.VMEM(weight.shape, F32),
            pltpu.VMEM(z_shape, BF16),
            pltpu.VMEM(z_shape, BF16),
            pltpu.VMEM((CX * CY, columns), F32),
            pltpu.VMEM((CX * CY, columns), F32),
            pltpu.VMEM((modes, L), F32),
            pltpu.VMEM((2, B, CX, R, L), F32),
            pltpu.VMEM((2, B, CX, R, L), F32),
            pltpu.VMEM((2, A, CX, R2, L), F32),
            pltpu.VMEM((2, A, CX, R2, L), F32),
            pltpu.VMEM((2, A, CX, R2, L), F32),
            pltpu.VMEM((2, A, CX, R2, L), F32),
            pltpu.VMEM((2, B, CX, R, L), F32),
            pltpu.VMEM((B, C + ROWS, L), F32),
            pltpu.VMEM((A, C + ROWS, L), F32),
            dma((2, B, CX)), dma((2, B, CX)),
            dma((2, A, steps)), dma((2, A, steps)),
            dma((2, A)), dma((2, A)),
            dma((2, B, steps)), dma((2, B, steps)),
            dma((B,)), dma((B,)),
            dma((A,)), dma((A,)),
            dma((3,)),
        ],
        compiler_params=pltpu.CompilerParams(
            collective_id=0, has_side_effects=True, vmem_limit_bytes=VMEM_BYTES
        ),
    )(field, cotangent, weight, point, bias.reshape(1, C), *made)
    results = pl.pallas_call(
        functools.partial(finish, (owned, KX, C, L)),
        out_shape=(
            jax.ShapeDtypeStruct(field.shape, F32),
            jax.ShapeDtypeStruct(field.shape, F32),
            jax.ShapeDtypeStruct(weight.shape, F32),
            jax.ShapeDtypeStruct((C, C), F32),
            jax.ShapeDtypeStruct((1, C), F32),
        ),
        in_specs=[vmem, vmem, far, far, vmem, vmem],
        out_specs=(far, far, far, vmem, vmem),
        scratch_shapes=[pltpu.VMEM(weight.shape, F32), dma((owned + 2,))],
        compiler_params=pltpu.CompilerParams(vmem_limit_bytes=VMEM_BYTES),
    )(spectrum, slopes, output, grad_field, grad_point, grad_bias)
    return (*results[:4], results[4].reshape(C))


def solution(mesh):
    placed = (P("gx", "gy", None), P("gx", "gy", None), P("gx", None, None, None, "gy"), P(), P())
    return jax.shard_map(
        functools.partial(shards, mesh.shape["gx"], mesh.shape["gy"]),
        mesh=mesh,
        in_specs=placed,
        out_specs=(
            P("gx", "gy", None),
            P("gx", "gy", None),
            P("gx", None, None, None, "gy"),
            P(),
            P(),
        ),
        check_vma=False,
    )
```

```python
import functools
import math

import jax
import jax.numpy as jnp
import ml_dtypes
import numpy as np
from jax import lax
from jax.experimental import pallas as pl
from jax.experimental.pallas import tpu as pltpu
from jax.sharding import PartitionSpec as P

F32 = jnp.float32
BF16 = jnp.bfloat16
MESH = pl.DeviceIdType.MESH
HIGHEST = lax.Precision.HIGHEST
WIDE = 256
ROWS = 8
VMEM_BYTES = 58 * 1024 * 1024


def phases(positions, length, modes, signed):
    index = np.arange(modes)
    frequency = np.where(index >= modes // 2, index - modes, index) if signed else index
    turns = np.mod(positions[:, None] * frequency[None, :], length) * (2.0 * math.pi / length)
    return np.cos(turns), np.sin(turns)


def halves(table):
    table = np.asarray(table, np.float32)
    high = table.astype(ml_dtypes.bfloat16)
    low = (table - high.astype(np.float32)).astype(ml_dtypes.bfloat16)
    return high, low


def thirds(table):
    high, low = halves(table)
    return np.concatenate([high, high, low], -1)


def tables(nx, ny, nz, kx, ky, kz, chan, owned, split_y):
    cos_z, sin_z = phases(np.arange(nz), nz, kz, False)
    eye = np.eye(chan)
    first = np.concatenate([np.kron(cos_z, eye), np.kron(-sin_z, eye)], 1)
    cos_y, sin_y = phases(np.arange(ny), ny, ky, True)
    cells = ny // split_y
    cos_y = cos_y.reshape(split_y, cells, ky).transpose(0, 2, 1)
    sin_y = sin_y.reshape(split_y, cells, ky).transpose(0, 2, 1)
    real = np.concatenate([cos_y, sin_y], 2)
    imag = np.concatenate([-sin_y, cos_y], 2)
    second = np.stack([real, imag], 2).reshape(split_y, 2 * ky, 2 * cells)
    cos_x, sin_x = phases(np.arange(nx), nx, kx, True)
    third = np.zeros((owned, 2, kx, nx, owned, 2))
    for q in range(owned):
        third[q, 0, :, :, q, 0] = cos_x.T
        third[q, 0, :, :, q, 1] = sin_x.T
        third[q, 1, :, :, q, 0] = -sin_x.T
        third[q, 1, :, :, q, 1] = cos_x.T
    third = third.reshape(owned * 2 * kx, nx * owned * 2)
    return (
        *halves(first),
        *halves(first.T),
        thirds(second),
        thirds(second.transpose(0, 2, 1)),
        *halves(third),
        *halves(third.T),
    )


def parts_of(value):
    high = value.astype(BF16)
    return high, (value - high.astype(F32)).astype(BF16)


def dot(left, right):
    return jnp.dot(left, right, preferred_element_type=F32)


def right_product(value, high_table, low_table):
    rows = value.shape[0]
    high, low = parts_of(value)
    both = dot(jnp.concatenate([high, low], 0), high_table)
    return both[:rows] + both[rows:] + dot(high, low_table)


def left_product(high_table, low_table, value):
    columns = value.shape[1]
    high, low = parts_of(value)
    both = dot(high_table, jnp.concatenate([high, low], 1))
    return both[:, :columns] + both[:, columns:] + dot(low_table, high)


def left_thirds(table, value):
    high, low = parts_of(value)
    return dot(table, jnp.concatenate([high, low, high], 0))


def exact(left, right, dims):
    return lax.dot_general(
        left, right, (dims, ((), ())), precision=HIGHEST, preferred_element_type=F32
    )


def iota(shape, axis):
    return lax.broadcasted_iota(jnp.int32, shape, axis)


def channel_tables(C, L):
    pick = (iota((C, L), 0) == iota((C, L), 1) % C).astype(F32)
    group = ((iota((2 * L, L), 0) % L) // C == iota((2 * L, L), 1) // C).astype(F32).astype(BF16)
    return pick, group


def grouped(high, low, group):
    return dot(jnp.concatenate([high, low], 1), group)


def widen(value, pick, group):
    C, L = pick.shape
    high, low = parts_of(value)
    pair = [
        (part.astype(F32)[:, None, :] * pick[None]).reshape(value.shape[0] * C, L).astype(BF16)
        for part in (high, low)
    ]
    return grouped(*pair, group).reshape(value.shape[0], C, L)


def finish(
    sizes, spectrum, slopes, output_in, field_in, point_in, bias_in,
    output, grad_field, grad_weight_out, grad_point, grad_bias, grad_weight, sem,
):
    owned, KX, C, L = sizes
    copies = []
    output[...] = output_in[...]
    grad_field[...] = field_in[...]
    grad_point[...] = point_in[...]
    grad_bias[...] = bias_in[...]
    pick, group = channel_tables(C, L)
    for q in range(owned):
        for p in range(0, KX, ROWS):
            at = q * 2 * KX + p
            s_real = widen(spectrum[at : at + ROWS], pick, group)
            s_imag = widen(spectrum[at + KX : at + KX + ROWS], pick, group)
            real = slopes[at : at + ROWS][:, None, :]
            imag = slopes[at + KX : at + KX + ROWS][:, None, :]
            grad_weight[q, p : p + ROWS, 0] = s_real * real + s_imag * imag
            grad_weight[q, p : p + ROWS, 1] = s_real * imag - s_imag * real
        copy = pltpu.make_async_copy(grad_weight.at[q], grad_weight_out.at[q], sem.at[q])
        copy.start()
        copies.append(copy)
    for copy in copies:
        copy.wait()


def kernel(
    sizes,
    field, cotangent, weight_in, point, bias,
    za_high, za_low, zs_high_in, zs_low_in, ya, ys, xa_high, xa_low, xs_high, xs_low,
    output, grad_field, spectrum, slopes, grad_point, grad_bias,
    weight, zs_high, zs_low, hidden_base, grad_hidden, mixed,
    rs_out, rs_in, xy_out, xy_in, yx_out, yx_in, gathered, total_y, total_x,
    rs_ss, rs_rs, xy_ss, xy_rs, yx_ss, yx_rs, ag_ss, ag_rs, ty_ss, ty_rs, tx_ss, tx_rs, local_sem,
):
    A, B, CX, CY, KX, KC, L, C, owned, cells, steps = sizes
    R2 = 2 * owned
    a = lax.axis_index("gx")
    b = lax.axis_index("gy")

    def peer_x(d):
        return lax.rem(a + d, A)

    def peer_y(d):
        return lax.rem(b + d, B)

    def place(gx, gy):
        return {"gx": gx, "gy": gy}

    def remote(src, dst, ss, rs, where):
        return pltpu.make_async_remote_copy(
            src_ref=src, dst_ref=dst, send_sem=ss, recv_sem=rs, device_id=where, device_id_type=MESH
        )

    barrier = pltpu.get_barrier_semaphore()
    for d in range(1, A):
        pl.semaphore_signal(barrier, inc=1, device_id=place(peer_x(d), b), device_id_type=MESH)
    for d in range(1, B):
        pl.semaphore_signal(barrier, inc=1, device_id=place(a, peer_y(d)), device_id_type=MESH)
    loads = [
        pltpu.make_async_copy(weight_in, weight, local_sem.at[0]),
        pltpu.make_async_copy(zs_high_in, zs_high, local_sem.at[1]),
        pltpu.make_async_copy(zs_low_in, zs_low, local_sem.at[2]),
    ]
    for load in loads:
        load.start()
    sends = []

    def analyse_columns(turn, rows, first):
        z = right_product(rows, za_high[...], za_low[...])
        for n in range(rows.shape[0] // CY):
            one = z[n * CY : (n + 1) * CY]
            y = left_thirds(ya[b], jnp.concatenate([one[:, :KC], one[:, KC:]], 0))
            for j in range(B):
                rs_out[turn, j, first + n] = y[:, j * L : (j + 1) * L]

    def scatter(turn, x):
        made = []
        for d in range(1, B):
            copy = remote(
                rs_out.at[turn, peer_y(d), x], rs_in.at[turn, d, x],
                rs_ss.at[turn, d, x], rs_rs.at[turn, d, x], place(a, peer_y(d)),
            )
            copy.start()
            made.append(copy)
        sends.extend(made)
        return made

    def sum_and_send(turn, first, count, arriving):
        for n in range(count):
            x = first + n
            total = rs_out[turn, b, x]
            for d, copy in enumerate(arriving[x], 1):
                copy.wait_recv()
                total = total + rs_in[turn, d, x]
            for s in range(A):
                xy_out[turn, s, x] = total[s * R2 : (s + 1) * R2]
        h = first // count
        made = []
        for d in range(1, A):
            copy = remote(
                xy_out.at[turn, peer_x(d), pl.ds(first, count)], xy_in.at[turn, a, pl.ds(first, count)],
                xy_ss.at[turn, d, h], xy_rs.at[turn, d, h], place(peer_x(d), b),
            )
            copy.start()
            made.append(copy)
        sends.extend(made)
        xy_in[turn, a, pl.ds(first, count)] = xy_out[turn, a, pl.ds(first, count)]
        return made

    def transform_x(turn, arriving):
        for copy in arriving:
            copy.wait_recv()
        if R2 % ROWS == 0:
            value = xy_in[turn].reshape(A * CX * R2, L)
        else:
            value = jnp.concatenate([xy_in[turn, s, x] for s in range(A) for x in range(CX)], 0)
        return left_product(xa_high[...], xa_low[...], value)

    def back_x(turn):
        value = left_product(xs_high[...], xs_low[...], mixed[...])
        for s in range(A):
            for x in range(CX):
                at = (s * CX + x) * R2
                yx_out[turn, s, x] = value[at : at + R2]
        made = []
        for d in range(1, A):
            copy = remote(
                yx_out.at[turn, peer_x(d)], yx_in.at[turn, a],
                yx_ss.at[turn, d], yx_rs.at[turn, d], place(peer_x(d), b),
            )
            copy.start()
            made.append(copy)
        sends.extend(made)
        yx_in[turn, a] = yx_out[turn, a]
        return made

    def gather(turn, arriving):
        for copy in arriving:
            copy.wait_recv()
        made = []
        count = CX // steps
        for h in range(steps):
            for x in range(h * count, (h + 1) * count):
                for s in range(A):
                    gathered[turn, b, x, s * R2 : (s + 1) * R2] = yx_in[turn, s, x]
            own = gathered.at[turn, b, pl.ds(h * count, count)]
            group = []
            for d in range(1, B):
                copy = remote(
                    own, own, ag_ss.at[turn, d, h], ag_rs.at[turn, d, h], place(a, peer_y(d))
                )
                copy.start()
                group.append(copy)
            sends.extend(group)
            made.append(group)
        return made

    def synthesise_columns(turn, first, count, arriving):
        for copy in arriving:
            copy.wait_recv()
        slabs = []
        for x in range(first, first + count):
            modes = jnp.concatenate([gathered[turn, j, x] for j in range(B)], 1)
            grid = left_thirds(ys[b], modes)
            slabs.append(jnp.concatenate([grid[:CY], grid[CY:]], 1))
        return right_product(jnp.concatenate(slabs, 0), zs_high[...], zs_low[...])

    fold = (iota((WIDE, C), 0) % C == iota((WIDE, C), 1)).astype(F32)
    fold_wide = (iota((WIDE, L), 0) % C == iota((WIDE, L), 1)).astype(F32)
    same = (iota((WIDE, WIDE), 0) // C == iota((WIDE, WIDE), 1) // C).astype(F32)
    pick, group = channel_tables(C, L)
    mode = b * (L // C) + iota((1, L), 1) // C
    factor = jnp.where(mode == 0, 1.0, 2.0).astype(F32) * (1.0 / cells)
    columns = field.shape[2]
    blocks = columns // WIDE

    def stacked(value):
        return jnp.concatenate([value[:, j * WIDE : (j + 1) * WIDE] for j in range(blocks)], 0)

    def unstacked(value):
        rows = value.shape[0] // blocks
        return jnp.concatenate([value[j * rows : (j + 1) * rows] for j in range(blocks)], 1)

    def pointwise(value, axis):
        table = exact(exact(fold, point[...], ((1,), (axis,))), fold, ((1,), (1,))) * same
        return unstacked(right_product(stacked(value), *parts_of(table)))

    signal = field[...].reshape(CX * CY, columns)
    count = CX // steps
    rows = count * CY
    arriving = []
    for h in range(steps):
        analyse_columns(0, signal[h * rows : (h + 1) * rows], h * count)
        if h == 0:
            pl.semaphore_wait(barrier, A + B - 2)
        arriving += [scatter(0, h * count + n) for n in range(count)]
    tiled = exact(bias[...], fold, ((1,), (1,)))
    hidden_base[...] = pointwise(signal, 0) + jnp.concatenate([tiled] * blocks, 1)
    moved = []
    for h in range(steps):
        moved += sum_and_send(0, h * count, count, arriving)
    spectrum[...] = transform_x(0, moved)
    loads[0].wait()
    per = KX // ROWS

    def place_of(t):
        q = t // per
        p = (t % per) * ROWS
        return q, p, pl.multiple_of(q * (2 * KX) + p, ROWS)

    def over_modes(step):
        many = max(n for n in (4, 2, 1) if (owned * per) % n == 0)

        def some(t, carry):
            for n in range(many):
                step(t * many + n)
            return carry

        lax.fori_loop(0, owned * per // many, some, 0)

    def mix(t):
        q, p, at = place_of(t)
        real = widen(spectrum[pl.ds(at, ROWS)], pick, group)
        imag = widen(spectrum[pl.ds(at + KX, ROWS)], pick, group)
        w_real = weight[q, pl.ds(p, ROWS), 0]
        w_imag = weight[q, pl.ds(p, ROWS), 1]
        mixed[pl.ds(at, ROWS)] = jnp.sum(real * w_real - imag * w_imag, 1) * factor
        mixed[pl.ds(at + KX, ROWS)] = jnp.sum(real * w_imag + imag * w_real, 1) * factor

    over_modes(mix)
    returned = gather(0, back_x(0))
    loads[1].wait()
    loads[2].wait()

    arriving = []
    for h in range(steps):
        rows = count * CY
        at = h * rows
        value = synthesise_columns(0, h * count, count, returned[h]) + hidden_base[at : at + rows]
        below = 0.5 * (1.0 + lax.erf(value * math.sqrt(0.5)))
        density = jnp.exp(-0.5 * value * value) * (1.0 / math.sqrt(2.0 * math.pi))
        output[h * count : (h + 1) * count] = (value * below).reshape(count, CY, columns)
        upper = cotangent[h * count : (h + 1) * count].reshape(rows, columns)
        slope = upper * (below + value * density)
        grad_hidden[at : at + rows] = slope
        analyse_columns(1, slope, h * count)
        arriving += [scatter(1, h * count + n) for n in range(count)]

    slope = grad_hidden[...]
    left = parts_of(stacked(field[...].reshape(CX * CY, columns)))
    right = parts_of(stacked(slope))

    def crossed(one, two):
        return lax.dot_general(one, two, (((0,), (0,)), ((), ())), preferred_element_type=F32)

    pairs = (crossed(left[0], right[0]) + crossed(left[0], right[1]) + crossed(left[1], right[0])) * same
    point_part = exact(exact(fold, pairs, ((0,), (0,))), fold_wide, ((1,), (0,)))
    bias_part = exact(jnp.sum(stacked(slope), 0, keepdims=True), fold_wide, ((1,), (0,)))
    total_y[b, 0:C] = point_part
    total_y[b, C : C + ROWS] = jnp.broadcast_to(bias_part, (ROWS, L))
    own = total_y.at[b]
    totals = []
    for d in range(1, B):
        copy = remote(own, own, ty_ss.at[d], ty_rs.at[d], place(a, peer_y(d)))
        copy.start()
        totals.append(copy)
    sends.extend(totals)
    hidden_base[...] = pointwise(slope, 1)

    moved = []
    for h in range(steps):
        moved += sum_and_send(1, h * count, count, arriving)
    for copy in totals:
        copy.wait_recv()
    total = total_y[0]
    for j in range(1, B):
        total = total + total_y[j]
    total_x[a] = total
    own = total_x.at[a]
    totals = []
    for d in range(1, A):
        copy = remote(own, own, tx_ss.at[d], tx_rs.at[d], place(peer_x(d), b))
        copy.start()
        totals.append(copy)
    sends.extend(totals)
    slopes[...] = transform_x(1, moved) * factor

    def unmix(t):
        q, p, at = place_of(t)
        real = slopes[pl.ds(at, ROWS)][:, None, :]
        imag = slopes[pl.ds(at + KX, ROWS)][:, None, :]
        w_real = weight[q, pl.ds(p, ROWS), 0]
        w_imag = weight[q, pl.ds(p, ROWS), 1]
        for term, to in ((real * w_real + imag * w_imag, at), (imag * w_real - real * w_imag, at + KX)):
            summed = grouped(*parts_of(term.reshape(ROWS * C, L)), group).reshape(ROWS, C, L)
            mixed[pl.ds(to, ROWS)] = jnp.sum(summed * pick[None], 1)

    over_modes(unmix)
    returned = gather(1, back_x(1))
    for copy in totals:
        copy.wait_recv()
    total = total_x[0]
    for s in range(1, A):
        total = total + total_x[s]
    total = total * (1.0 / math.sqrt(cells))
    grad_point[...] = total[0:C, 0:C]
    grad_bias[...] = total[C : C + 1, 0:C]
    for h in range(steps):
        rows = count * CY
        at = h * rows
        value = synthesise_columns(1, h * count, count, returned[h]) + hidden_base[at : at + rows]
        grad_field[h * count : (h + 1) * count] = value.reshape(count, CY, columns)
    for copy in sends:
        copy.wait_send()


def shards(A, B, field, cotangent, weight, point, bias):
    CX, CY, columns = field.shape
    C = point.shape[0]
    owned, KX, _, _, L = weight.shape
    depth = L // C
    KY, KZ, NZ = owned * A, depth * B, columns // C
    NX, NY = CX * A, CY * B
    cells = NX * NY * NZ
    R, R2, KC = 2 * KY, 2 * owned, KZ * C
    steps = 2 if CX % 2 == 0 else 1
    made = [jnp.asarray(t) for t in tables(NX, NY, NZ, KX, KY, KZ, C, owned, B)]
    sizes = (A, B, CX, CY, KX, KC, L, C, owned, cells, steps)
    vmem = pl.BlockSpec(memory_space=pltpu.VMEM)
    far = pl.BlockSpec(memory_space=pl.ANY)
    dma = pltpu.SemaphoreType.DMA
    z_shape = made[2].shape
    modes = owned * 2 * KX
    output, grad_field, spectrum, slopes, grad_point, grad_bias = pl.pallas_call(
        functools.partial(kernel, sizes),
        out_shape=(
            jax.ShapeDtypeStruct(field.shape, F32),
            jax.ShapeDtypeStruct(field.shape, F32),
            jax.ShapeDtypeStruct((modes, L), F32),
            jax.ShapeDtypeStruct((modes, L), F32),
            jax.ShapeDtypeStruct((C, C), F32),
            jax.ShapeDtypeStruct((1, C), F32),
        ),
        in_specs=[vmem, vmem, far, vmem, vmem, vmem, vmem, far, far] + [vmem] * 6,
        out_specs=(vmem,) * 6,
        scratch_shapes=[
            pltpu.VMEM(weight.shape, F32),
            pltpu.VMEM(z_shape, BF16),
            pltpu.VMEM(z_shape, BF16),
            pltpu.VMEM((CX * CY, columns), F32),
            pltpu.VMEM((CX * CY, columns), F32),
            pltpu.VMEM((modes, L), F32),
            pltpu.VMEM((2, B, CX, R, L), F32),
            pltpu.VMEM((2, B, CX, R, L), F32),
            pltpu.VMEM((2, A, CX, R2, L), F32),
            pltpu.VMEM((2, A, CX, R2, L), F32),
            pltpu.VMEM((2, A, CX, R2, L), F32),
            pltpu.VMEM((2, A, CX, R2, L), F32),
            pltpu.VMEM((2, B, CX, R, L), F32),
            pltpu.VMEM((B, C + ROWS, L), F32),
            pltpu.VMEM((A, C + ROWS, L), F32),
            dma((2, B, CX)), dma((2, B, CX)),
            dma((2, A, steps)), dma((2, A, steps)),
            dma((2, A)), dma((2, A)),
            dma((2, B, steps)), dma((2, B, steps)),
            dma((B,)), dma((B,)),
            dma((A,)), dma((A,)),
            dma((3,)),
        ],
        compiler_params=pltpu.CompilerParams(
            collective_id=0, has_side_effects=True, vmem_limit_bytes=VMEM_BYTES
        ),
    )(field, cotangent, weight, point, bias.reshape(1, C), *made)
    results = pl.pallas_call(
        functools.partial(finish, (owned, KX, C, L)),
        out_shape=(
            jax.ShapeDtypeStruct(field.shape, F32),
            jax.ShapeDtypeStruct(field.shape, F32),
            jax.ShapeDtypeStruct(weight.shape, F32),
            jax.ShapeDtypeStruct((C, C), F32),
            jax.ShapeDtypeStruct((1, C), F32),
        ),
        in_specs=[vmem] * 6,
        out_specs=(vmem, vmem, far, vmem, vmem),
        scratch_shapes=[pltpu.VMEM(weight.shape, F32), dma((owned,))],
        compiler_params=pltpu.CompilerParams(vmem_limit_bytes=VMEM_BYTES),
    )(spectrum, slopes, output, grad_field, grad_point, grad_bias)
    return (*results[:4], results[4].reshape(C))


def solution(mesh):
    placed = (P("gx", "gy", None), P("gx", "gy", None), P("gx", None, None, None, "gy"), P(), P())
    return jax.shard_map(
        functools.partial(shards, mesh.shape["gx"], mesh.shape["gy"]),
        mesh=mesh,
        in_specs=placed,
        out_specs=(
            P("gx", "gy", None),
            P("gx", "gy", None),
            P("gx", None, None, None, "gy"),
            P(),
            P(),
        ),
        check_vma=False,
    )
```
